512 devices in a mesh: lev: 4 (over y), lat: 4 (over x), lon: 32 (over z, core).
Axes of the slice: x: 4, y: 4, z: 16, core: 2. Of those that a mesh axis runs over, the one named last changes fastest.
Arguments:
- anomalies: bfloat16 [64, 512, 2560], P('lat', 'lon', 'lev'), may hold values from -6 to 6
- error_grad: float32 [64, 512, 32], P('lat', 'lon', 'lev'), may hold values from -288 to 288
- obs_lat: float32 [4, 32, 2048], P('lat', 'lon'), may hold values from 0 to 16
- obs_lon: float32 [4, 32, 2048], P('lat', 'lon'), may hold values from 0 to 16
- obs_level: int32 [4, 32, 2048], P('lat', 'lon'), may hold values from 0 to 31
- obs_count: int32 [4, 32], P('lat', 'lon'), may hold values from 512 to 2048, as said below
- obs_pert: bfloat16 [4, 32, 80, 2048], P('lat', 'lon'), may hold values from -6 to 6
- innovation: float32 [4, 32, 2048], P('lat', 'lon'), may hold values from -6 to 6
- inv_error: float32 [4, 32, 2048], P('lat', 'lon'), may hold values from 0.25 to 4
Outputs:
- impact: float32 [4, 32, 2048], P('lat', 'lon')
The draws below stay inside these ranges and needn't reach their ends.
Inputs may be any that keep to these rules, and one draw needn't show every extreme that they name: Live observations occupy the first obs_count slots of a tile's block; entries of other slots are arbitrary. Exactly one tile holds 2048 observations; the others hold from 512 to 1280.
All inputs are finite; a program needn't handle non-finite values.
Results may differ from the reference program's by a relative error of at most 0.0041.
Values may be sent and summed in bfloat16 or wider, within the bound.
A program may use at most 64 MiB of HBM per device.

```python
import math
import jax
import jax.numpy as jnp
from jax import lax

K = 80
LEV_DEV = 8
TY = 16
TX = 16
OBS_CAP = 2048
LEVELS = 32
NY = 64
NX = 512
TILES_Y = 4
TILES_X = 32


def draw_obs_count(key, part):
    key = jax.random.fold_in(key, 11)
    first, second = jax.random.split(key)
    total = TILES_Y * TILES_X
    counts = jax.random.randint(first, (total,), OBS_CAP // 4, OBS_CAP * 5 // 8 + 1, dtype=jnp.int32)
    busiest = jax.random.randint(second, (), 0, total, dtype=jnp.int32)
    counts = jnp.where(jnp.arange(total, dtype=jnp.int32) == busiest, OBS_CAP, counts)
    return counts.reshape(TILES_Y, TILES_X).astype(jnp.int32)


def draw_error_grad(key, part):
    key = jax.random.fold_in(key, 13)
    values = jax.random.truncated_normal(key, -6.0, 6.0, (NY, NX, LEVELS), jnp.float32)
    return values


def draw_obs_lon(key, part):
    key = jax.random.fold_in(key, 17)
    first = jax.random.fold_in(key, 0)
    shape = (TILES_Y, TILES_X, OBS_CAP)
    return jax.random.uniform(first, shape, jnp.float32, 0.0, TX)


def set_ends(drawn, own_key, low, top_value):
    longest = drawn.shape.index(max(drawn.shape))
    spots = []
    for shift in (0, 1):
        where = [jax.random.randint(jax.random.fold_in(own_key, axis), (), 0, length) for axis, length in enumerate(drawn.shape)]
        where[longest] = (where[longest] + shift) % drawn.shape[longest]
        spots.append(tuple(where))
    return drawn.at[spots[0]].set(low).at[spots[1]].set(top_value)


def shard_levels(stream_key, shape, cuts, least, largest):
    def one(dim, shards_of):
        steps = jax.random.uniform(jax.random.fold_in(jax.random.fold_in(stream_key, 6), dim), (shards_of,), jnp.float32, least / len(cuts), largest / len(cuts))
        return jnp.repeat(jnp.exp(steps), shape[dim] // shards_of).reshape((-1,) + (1,) * (len(shape) - dim - 1))

    factor_of = one(*cuts[0])
    for cut in cuts[1:]:
        factor_of = factor_of * one(*cut)
    return factor_of


def centred(rng, extent, deviation, most, shards=(), kind=jnp.bfloat16):
    array = deviation * jax.random.normal(rng, extent, jnp.float32)
    if shards:
        array = array * shard_levels(rng, extent, shards, -0.22, 0.18)
    return jnp.clip(array, -most, most).astype(kind)


def setup_inputs(seed: int = 0) -> dict:
    streams_of = jax.random.split(jax.random.key(seed), 10)
    anomalies = centred(streams_of[0], (NY, NX, LEVELS * K), 1.0, 6.0, ((0, 4), (1, 32), (2, 4)))
    error_grad = draw_error_grad(jax.random.fold_in(streams_of[9], 71), 0)
    obs_lat = jnp.clip(16.0 * jax.random.uniform(streams_of[2], (TILES_Y, TILES_X, OBS_CAP), jnp.float32) ** shard_levels(streams_of[2], (TILES_Y, TILES_X, OBS_CAP), ((0, 4), (1, 32)), -0.2, 0.2), 0.0, 16.0)
    obs_lon = draw_obs_lon(jax.random.fold_in(streams_of[9], 71), 0)
    obs_level = set_ends(jax.random.randint(streams_of[4], (TILES_Y, TILES_X, OBS_CAP), 0, LEVELS), jax.random.fold_in(streams_of[4], 1), 0, LEVELS - 1).astype(jnp.int32)
    obs_count = draw_obs_count(jax.random.fold_in(streams_of[9], 71), 0)
    obs_pert = centred(streams_of[6], (TILES_Y, TILES_X, K, OBS_CAP), 1.0, 6.0, ((0, 4), (1, 32)))
    innovation = centred(streams_of[7], (TILES_Y, TILES_X, OBS_CAP), 1.0, 6.0, ((0, 4), (1, 32)), jnp.float32)
    inv_error = jnp.clip(jnp.exp(math.log(4.0) - 2.7725887 * jax.random.uniform(streams_of[8], (TILES_Y, TILES_X, OBS_CAP), jnp.float32) ** shard_levels(streams_of[8], (TILES_Y, TILES_X, OBS_CAP), ((0, 4), (1, 32)), -0.2, 0.2)), 0.25, 4.0)
    return {"anomalies": anomalies, "error_grad": error_grad, "obs_lat": obs_lat, "obs_lon": obs_lon, "obs_level": obs_level, "obs_count": obs_count, "obs_pert": obs_pert, "innovation": innovation, "inv_error": inv_error}


def taper(dist, support):
    r = 2.0 * dist / support
    inner = (((-0.25 * r + 0.5) * r + 0.625) * r - 5.0 / 3.0) * r * r + 1.0
    safe_r = jnp.maximum(r, 1.0)
    outer = ((((r / 12.0 - 0.5) * r + 0.625) * r + 5.0 / 3.0) * r - 5.0) * r + 4.0 - 2.0 / (3.0 * safe_r)
    return jnp.where(r <= 1.0, inner, jnp.where(r < 2.0, outer, 0.0))

def vertical_weights(levels_obs, count, level_ids, support):
    dist = jnp.abs(levels_obs[None, :] - level_ids[:, None]).astype(jnp.float32)
    live = (jnp.arange(levels_obs.shape[0], dtype=jnp.int32) < count).astype(jnp.float32)
    return taper(dist, support) * live[None, :]

def block_sums(cells, pos_y, pos_x, weights, pert, row0, col0, rim):
    rows, cols, width = cells.shape
    slots = pos_y.shape[0]
    depth = weights.shape[0]
    members = pert.shape[0]
    blk = min(512, slots)
    flat = cells.reshape(rows * cols, width).astype(jnp.float32)
    grid_y = jnp.arange(rows, dtype=jnp.float32) + (row0 + 0.5)
    grid_x = jnp.arange(cols, dtype=jnp.float32) + (col0 + 0.5)

    def one_block(start):
        py = lax.dynamic_slice_in_dim(pos_y, start, blk, 0)
        px = lax.dynamic_slice_in_dim(pos_x, start, blk, 0)
        wblk = lax.dynamic_slice_in_dim(weights, start, blk, 1)
        pblk = lax.dynamic_slice_in_dim(pert, start, blk, 1)
        delta_y = py[:, None] - grid_y[None, :]
        delta_x = px[:, None] - grid_x[None, :]
        dist = jnp.sqrt(delta_y[:, :, None] ** 2 + delta_x[:, None, :] ** 2)
        rho = taper(dist, rim).astype(jnp.bfloat16).reshape(blk, rows * cols)
        proj = jnp.dot(rho.astype(jnp.float32), flat, precision=lax.Precision.HIGHEST)
        proj = proj.reshape(blk, depth, members)
        inner = jnp.einsum('blk,kb->bl', proj, pblk.astype(jnp.float32), precision=lax.Precision.HIGHEST)
        return lax.optimization_barrier(jnp.sum(inner * wblk.T, axis=1))
    starts = jnp.arange(slots // blk, dtype=jnp.int32) * blk
    return lax.map(one_block, starts).reshape(slots)

def reference(anomalies, error_grad, obs_lat, obs_lon, obs_level, obs_count, obs_pert, innovation, inv_error):
    rim = min(TY, TX) // 2
    tiles = TILES_Y * TILES_X
    weighted = (anomalies.reshape(NY, NX, LEVELS, K).astype(jnp.float32) * error_grad[..., None]).astype(jnp.bfloat16)
    weighted = weighted.reshape(NY, NX, LEVELS * K)
    padded = jnp.concatenate([weighted[:, NX - rim:], weighted, weighted[:, :rim]], axis=1)
    padded = jnp.pad(padded, ((rim, rim), (0, 0), (0, 0)))
    level_ids = jnp.arange(LEVELS, dtype=jnp.int32)
    lat_all = obs_lat.reshape(tiles, OBS_CAP)
    lon_all = obs_lon.reshape(tiles, OBS_CAP)
    level_all = obs_level.reshape(tiles, OBS_CAP)
    count_all = obs_count.reshape(tiles)
    pert_all = obs_pert.reshape(tiles, K, OBS_CAP)
    innov_all = innovation.reshape(tiles, OBS_CAP)
    inv_all = inv_error.reshape(tiles, OBS_CAP)

    def one_tile(tile):
        tile_y = (tile // TILES_X).astype(jnp.int32)
        tile_x = (tile % TILES_X).astype(jnp.int32)
        start_zero = jnp.zeros((), jnp.int32)
        block = lax.dynamic_slice(padded, (tile_y * TY, tile_x * TX, start_zero), (TY + 2 * rim, TX + 2 * rim, LEVELS * K))
        weights = vertical_weights(level_all[tile], count_all[tile], level_ids, LEV_DEV)
        sens = block_sums(block, lat_all[tile], lon_all[tile], weights, pert_all[tile], -rim, -rim, rim)
        return innov_all[tile] * inv_all[tile] * sens / (K - 1.0)
    result = lax.map(one_tile, jnp.arange(tiles, dtype=jnp.int32))
    return result.reshape(TILES_Y, TILES_X, OBS_CAP)
```

```python
import functools

import jax
import jax.numpy as jnp
from jax import lax
from jax.experimental import pallas as pl
from jax.experimental.pallas import tpu as pltpu
from jax.sharding import PartitionSpec as P

MESH = pl.DeviceIdType.MESH
LANES = 128
HALF = 8
QUAD = HALF * HALF
OWN, SIDE, BAND, CORNER = range(4)


def vertical_taper(dist, support):
    r = 2.0 * dist / support
    inner = (((-0.25 * r + 0.5) * r + 0.625) * r - 5.0 / 3.0) * r * r + 1.0
    safe_r = jnp.maximum(r, 1.0)
    outer = (
        ((((r / 12.0 - 0.5) * r + 0.625) * r + 5.0 / 3.0) * r - 5.0) * r
        + 4.0
        - 2.0 / (3.0 * safe_r)
    )
    return jnp.where(r <= 1.0, inner, jnp.where(r < 2.0, outer, 0.0))


def taper_of_square(q):
    s = lax.rsqrt(q)
    r = q * s
    inner = 1.0 + q * (0.5 * q - 5.0 / 3.0) + (q * r) * (0.625 - 0.25 * q)
    t = jnp.maximum(2.0 - r, 0.0)
    t = t * t
    outer = (t * t) * ((r + 2.0) * (1.0 / 12.0) - s * (1.0 / 24.0))
    return jnp.where(r <= 1.0, inner, outer)


def wrapped(i, n):
    return lax.rem(i + n, n)


def kernel(
    sizes,
    anomalies,
    error_grad,
    obs_lat,
    obs_lon,
    obs_level,
    obs_count,
    obs_pert,
    innovation,
    inv_error,
    impact,
    cells,
    terms,
    rho,
    total,
    parts,
    send_sem,
    recv_sem,
    lev_send,
    lev_recv,
):
    levs, lats, lons = sizes
    depth = error_grad.shape[1]
    width = cells.shape[3]
    members = width // depth
    slots = terms.shape[1]
    tile = min(256, slots)
    lev, lat, lon = (lax.axis_index(a) for a in ("lev", "lat", "lon"))
    below, above = wrapped(lat + 1, lats), wrapped(lat - 1, lats)
    right, left = wrapped(lon + 1, lons), wrapped(lon - 1, lons)

    barrier = pltpu.get_barrier_semaphore()
    greeted = [{"lat": below}, {"lat": above}, {"lon": right}, {"lon": left}]
    greeted += [{"lev": wrapped(lev + k, levs)} for k in range(1, levs)]
    for other in greeted:
        pl.semaphore_signal(barrier, inc=1, device_id=other, device_id_type=MESH)

    lane = lax.broadcasted_iota(jnp.int32, (2 * HALF, LANES), 1)

    def weigh(pair, carry):
        halves = []
        for step in range(2):
            y = pair * 2 + step
            grad = error_grad[pl.ds(pl.multiple_of(y * 2 * HALF, 2 * HALF), 2 * HALF), :]
            spread = [jnp.broadcast_to(grad[:, m : m + 1], lane.shape) for m in range(depth)]
            pieces = []
            for start in range(0, width, LANES):
                lowest, highest = start // members, (start + LANES - 1) // members
                factor = spread[lowest]
                for m in range(lowest + 1, highest + 1):
                    factor = jnp.where(lane >= m * members - start, spread[m], factor)
                pieces.append(anomalies[y, :, start : start + LANES].astype(jnp.float32) * factor)
            halves.append(pieces)
        qy, row = pair // 4, pl.multiple_of((pair % 4) * 2 * HALF, 2 * HALF)
        for qx in range(2):
            for n, (top, bottom) in enumerate(zip(*halves)):
                both = jnp.concatenate(
                    [top[qx * HALF : (qx + 1) * HALF], bottom[qx * HALF : (qx + 1) * HALF]], axis=0
                )
                cells[OWN, qx * 2 + qy, pl.ds(row, 2 * HALF), n * LANES : (n + 1) * LANES] = (
                    both.astype(jnp.bfloat16)
                )
        return carry

    lax.fori_loop(0, HALF, weigh, 0)

    pl.semaphore_wait(barrier, len(greeted))

    def copy(src, dst, sem, device):
        return pltpu.make_async_remote_copy(
            src_ref=src,
            dst_ref=dst,
            send_sem=send_sem.at[sem],
            recv_sem=recv_sem.at[sem],
            device_id=device,
            device_id_type=MESH,
        )

    first = lax.rem(lon, 2)
    order = (first, 1 - first)

    def to_below(q):
        return copy(cells.at[OWN, q * 2 + 1], cells.at[BAND, q], q, {"lat": below})

    def to_above(q):
        return copy(cells.at[OWN, q * 2], cells.at[BAND, 2 + q], 2 + q, {"lat": above})

    def forward(d, q):
        aside = wrapped(lon + 2 * q - 1, lons)
        return copy(
            cells.at[BAND, d * 2 + q],
            cells.at[CORNER, d * 2 + 1 - q],
            6 + d * 2 + 1 - q,
            {"lon": aside},
        )

    to_right = copy(cells.at[OWN, pl.ds(2, 2)], cells.at[SIDE, pl.ds(0, 2)], 4, {"lon": right})
    to_left = copy(cells.at[OWN, pl.ds(0, 2)], cells.at[SIDE, pl.ds(2, 2)], 5, {"lon": left})
    to_below(order[0]).start()
    to_above(order[0]).start()
    to_right.start()
    to_left.start()
    to_below(order[1]).start()
    to_above(order[1]).start()

    def make_terms(n, carry):
        at = pl.ds(pl.multiple_of(n * tile, tile), tile)
        level = lax.broadcasted_iota(jnp.int32, (depth, tile), 0) + lev * depth
        slot = lax.broadcasted_iota(jnp.int32, (depth, tile), 1) + n * tile
        away = jnp.abs(obs_level[:, at] - level).astype(jnp.float32)
        live = (slot < obs_count[0, 0]).astype(jnp.float32)
        vertical = vertical_taper(away, depth) * live
        pert = obs_pert[:, at].astype(jnp.float32)
        for m in range(depth):
            terms[m * members : (m + 1) * members, at] = (pert * vertical[m : m + 1]).astype(
                jnp.bfloat16
            )
        return carry

    lax.fori_loop(0, slots // tile, make_terms, 0)

    def offset_x(at, side):
        centre = (lax.broadcasted_iota(jnp.int32, (HALF, tile), 0) + side * HALF).astype(jnp.float32)
        return (obs_lon[:, at] - (centre + (0.5 - HALF))) * (2.0 / HALF)

    def make_rho(n, carry):
        at = pl.ds(pl.multiple_of(n * tile, tile), tile)
        squares = []
        for side in range(2):
            dx = offset_x(at, side)
            dx = jnp.where(dx < 2.0, dx, dx - 4.0)
            squares.append(dx * dx + 1e-30)
        for j in range(2 * HALF):
            dy = (obs_lat[:, at] - (j + 0.5 - HALF)) * (2.0 / HALF)
            near = dy < 2.0
            dy = jnp.where(near, dy, dy - 4.0)
            dy2 = jnp.broadcast_to(dy * dy, (HALF, tile))
            near = jnp.broadcast_to(jnp.where(near, 1.0, 0.0), (HALF, tile)) > 0.5
            for side in range(2):
                value = taper_of_square(dy2 + squares[side])
                cols = slice(side * HALF, (side + 1) * HALF)
                rho[0, j, cols, at] = jnp.where(near, value, 0.0)
                rho[1, j, cols, at] = jnp.where(near, 0.0, value)
        return carry

    lax.fori_loop(0, slots // tile, make_rho, 0)

    total[...] = jnp.zeros_like(total)

    def add_piece(piece, quads):
        def body(n, carry):
            at = pl.ds(pl.multiple_of(n * tile, tile), tile)
            near = [offset_x(at, side) < 2.0 for side in range(2)]
            weights = cells[piece].reshape(len(quads) * QUAD, width)
            both = jnp.dot(weights, terms[:, at], preferred_element_type=jnp.float32)
            acc = total[:, at]
            for n_quad, (row, col) in enumerate(quads):
                a, j, b, i = row // 2, row % 2, col // 2, col % 2
                part = both[n_quad * QUAD : (n_quad + 1) * QUAD].reshape(HALF, HALF, tile)
                part = part * rho[a, j * HALF : (j + 1) * HALF, i * HALF : (i + 1) * HALF, at]
                part = jnp.sum(part, axis=0)
                keep = near[i] if b == 0 else jnp.logical_not(near[i])
                if row == 0:
                    keep = jnp.logical_and(keep, lat > 0)
                elif row == 3:
                    keep = jnp.logical_and(keep, lat < lats - 1)
                acc = acc + jnp.where(keep, part, 0.0)
            total[:, at] = acc
            return carry

        lax.fori_loop(0, slots // tile, body, 0)

    to_below(order[0]).wait_recv()
    forward(0, order[0]).start()
    to_above(order[0]).wait_recv()
    forward(1, order[0]).start()
    add_piece(OWN, [(1, 1), (2, 1), (1, 2), (2, 2)])
    to_below(order[1]).wait_recv()
    forward(0, order[1]).start()
    to_above(order[1]).wait_recv()
    forward(1, order[1]).start()
    to_right.wait_recv()
    to_left.wait_recv()
    add_piece(SIDE, [(1, 0), (2, 0), (1, 3), (2, 3)])
    add_piece(BAND, [(0, 1), (0, 2), (3, 1), (3, 2)])
    for d in range(2):
        for q in order:
            forward(d, q).wait_recv()
    add_piece(CORNER, [(0, 0), (0, 3), (3, 0), (3, 3)])

    parts[lev] = jnp.sum(total[...], axis=0, keepdims=True)
    swaps = []
    for k in range(1, levs):
        swaps.append(
            pltpu.make_async_remote_copy(
                src_ref=parts.at[lev],
                dst_ref=parts.at[lev],
                send_sem=lev_send.at[k - 1],
                recv_sem=lev_recv.at[k - 1],
                device_id={"lev": wrapped(lev + k, levs)},
                device_id_type=MESH,
            )
        )
        swaps[-1].start()
    for swap in swaps:
        swap.wait_recv()
    value = parts[0]
    for k in range(1, levs):
        value = value + parts[k]
    impact[...] = innovation[...] * inv_error[...] * value / (members - 1.0)

    for swap in swaps:
        swap.wait_send()
    to_right.wait_send()
    to_left.wait_send()
    for q in order:
        to_below(q).wait_send()
        to_above(q).wait_send()
        for d in range(2):
            forward(d, q).wait_send()


def per_device(
    sizes,
    anomalies,
    error_grad,
    obs_lat,
    obs_lon,
    obs_level,
    obs_count,
    obs_pert,
    innovation,
    inv_error,
):
    rows, cols, width = anomalies.shape
    depth = error_grad.shape[2]
    members, slots = obs_pert.shape[2:]
    vmem = pl.BlockSpec(memory_space=pltpu.VMEM)
    in_specs = [vmem] * 9
    in_specs[5] = pl.BlockSpec(memory_space=pltpu.SMEM)
    flat = (1, slots)
    impact = pl.pallas_call(
        functools.partial(kernel, sizes),
        out_shape=jax.ShapeDtypeStruct(flat, jnp.float32),
        in_specs=in_specs,
        out_specs=vmem,
        scratch_shapes=[
            pltpu.VMEM((4, 4, QUAD, width), jnp.bfloat16),
            pltpu.VMEM((width, slots), jnp.bfloat16),
            pltpu.VMEM((2, rows, cols, slots), jnp.float32),
            pltpu.VMEM((HALF, slots), jnp.float32),
            pltpu.VMEM((sizes[0], 1, slots), jnp.float32),
            pltpu.SemaphoreType.DMA((10,)),
            pltpu.SemaphoreType.DMA((10,)),
            pltpu.SemaphoreType.DMA((sizes[0] - 1,)),
            pltpu.SemaphoreType.DMA((sizes[0] - 1,)),
        ],
        compiler_params=pltpu.CompilerParams(
            collective_id=0, has_side_effects=True, vmem_limit_bytes=48 * 1024 * 1024
        ),
        cost_estimate=pl.CostEstimate(
            flops=2 * 4 * rows * cols * width * slots, bytes_accessed=4 * 10**6, transcendentals=0
        ),
    )(
        anomalies,
        error_grad.reshape(rows * cols, depth),
        obs_lat.reshape(flat),
        obs_lon.reshape(flat),
        obs_level.reshape(flat),
        obs_count,
        obs_pert.reshape(members, slots),
        innovation.reshape(flat),
        inv_error.reshape(flat),
    )
    return impact.reshape(1, 1, slots)


def solution(mesh):
    sizes = tuple(mesh.shape[a] for a in ("lev", "lat", "lon"))
    tiles = P("lat", "lon", None)
    placed = (
        P("lat", "lon", "lev"),
        P("lat", "lon", "lev"),
        tiles,
        tiles,
        tiles,
        P("lat", "lon"),
        P("lat", "lon", None, None),
        tiles,
        tiles,
    )
    return jax.shard_map(
        functools.partial(per_device, sizes),
        mesh=mesh,
        in_specs=placed,
        out_specs=tiles,
        check_vma=False,
    )
```

```python
import functools

import jax
import jax.numpy as jnp
from jax import lax
from jax.experimental import pallas as pl
from jax.experimental.pallas import tpu as pltpu
from jax.sharding import PartitionSpec as P

MESH = pl.DeviceIdType.MESH
LANES = 128
HALF = 8
QUAD = HALF * HALF
OWN, BAND, RIGHT, LEFT = range(4)


def vertical_taper(dist, support):
    r = 2.0 * dist / support
    inner = (((-0.25 * r + 0.5) * r + 0.625) * r - 5.0 / 3.0) * r * r + 1.0
    safe_r = jnp.maximum(r, 1.0)
    outer = (
        ((((r / 12.0 - 0.5) * r + 0.625) * r + 5.0 / 3.0) * r - 5.0) * r
        + 4.0
        - 2.0 / (3.0 * safe_r)
    )
    return jnp.where(r <= 1.0, inner, jnp.where(r < 2.0, outer, 0.0))


def taper_of_square(q):
    s = lax.rsqrt(q)
    r = q * s
    inner = 1.0 + q * (0.5 * q - 5.0 / 3.0) + (q * r) * (0.625 - 0.25 * q)
    t = jnp.maximum(2.0 - r, 0.0)
    t = t * t
    outer = (t * t) * ((r + 2.0) * (1.0 / 12.0) - s * (1.0 / 24.0))
    return jnp.where(r <= 1.0, inner, outer)


def wrapped(i, n):
    return lax.rem(i + n, n)


def kernel(
    sizes,
    anomalies_in,
    error_grad_in,
    obs_lat_in,
    obs_lon_in,
    obs_level_in,
    obs_count_in,
    obs_pert_in,
    innovation_in,
    inv_error_in,
    impact,
    anomalies,
    error_grad,
    obs_lat,
    obs_lon,
    obs_level,
    obs_count,
    obs_pert,
    innovation,
    inv_error,
    cells,
    terms,
    rho,
    total,
    parts,
    in_sem,
    send_sem,
    recv_sem,
    lev_send,
    lev_recv,
):
    levs, lats, lons = sizes
    rows, depth, cols = error_grad.shape
    width = cells.shape[3]
    members = width // depth
    slots = terms.shape[1]
    tile = min(256, slots)
    lev, lat, lon = (lax.axis_index(a) for a in ("lev", "lat", "lon"))
    below, above = wrapped(lat + 1, lats), wrapped(lat - 1, lats)
    right, left = wrapped(lon + 1, lons), wrapped(lon - 1, lons)

    loads = [
        pltpu.make_async_copy(src, dst, in_sem.at[n])
        for n, (src, dst) in enumerate(
            (
                (error_grad_in, error_grad),
                (anomalies_in, anomalies),
                (obs_level_in, obs_level),
                (obs_count_in, obs_count),
                (obs_pert_in, obs_pert),
                (obs_lat_in, obs_lat),
                (obs_lon_in, obs_lon),
                (innovation_in, innovation),
                (inv_error_in, inv_error),
            )
        )
    ]
    for load in loads:
        load.start()

    barrier = pltpu.get_barrier_semaphore()
    greeted = [{"lat": below}, {"lat": above}, {"lon": right}, {"lon": left}]
    greeted += [{"lat": n, "lon": m} for n in (below, above) for m in (right, left)]
    greeted += [{"lev": wrapped(lev + k, levs)} for k in range(1, levs)]
    for other in greeted:
        pl.semaphore_signal(barrier, inc=1, device_id=other, device_id_type=MESH)

    pairs = rows * depth
    level_of = lax.broadcasted_iota(jnp.int32, (pairs, width), 0) % depth * members
    lane = lax.broadcasted_iota(jnp.int32, (pairs, width), 1)
    inside = jnp.logical_and(lane >= level_of, lane < level_of + members)
    ones = jnp.where(inside, 1.0, 0.0).astype(jnp.bfloat16)
    ones = jnp.concatenate([ones] * 3, axis=0)
    row_of = lax.broadcasted_iota(jnp.int32, (HALF, pairs), 1) // depth
    loads[0].wait()
    rest = error_grad[...].reshape(pairs, cols).T
    grads = []
    for _ in range(3):
        grads.append(rest.astype(jnp.bfloat16).astype(jnp.float32))
        rest = rest - grads[-1]

    def weigh(qx):
        half = slice(qx * HALF, (qx + 1) * HALF)
        wide = [
            jnp.concatenate([jnp.where(row_of == y, grad[half], 0.0) for y in range(rows)], axis=0)
            for grad in grads
        ]
        wide = jnp.concatenate(wide, axis=1).astype(jnp.bfloat16)
        spread = jnp.dot(wide, ones, preferred_element_type=jnp.float32)
        for y in range(0, rows, 2):
            both = [anomalies[n].astype(jnp.float32)[half] for n in (y, y + 1)]
            both = jnp.concatenate(both, axis=0) * spread[y * HALF : (y + 2) * HALF]
            at = y % HALF * HALF
            cells[OWN, qx * 2 + y // HALF, at : at + 2 * HALF] = both.astype(jnp.bfloat16)

    def copy(sem, quads, piece, place, device):
        return pltpu.make_async_remote_copy(
            src_ref=cells.at[OWN, quads],
            dst_ref=cells.at[piece, place],
            send_sem=send_sem.at[sem],
            recv_sem=recv_sem.at[sem],
            device_id=device,
            device_id_type=MESH,
        )

    to_right = [
        copy(0, pl.ds(2, 2), LEFT, pl.ds(0, 2), {"lon": right}),
        copy(1, 3, LEFT, 2, {"lat": below, "lon": right}),
        copy(2, 2, LEFT, 3, {"lat": above, "lon": right}),
    ]
    to_left = [
        copy(3, pl.ds(0, 2), RIGHT, pl.ds(0, 2), {"lon": left}),
        copy(4, 1, RIGHT, 2, {"lat": below, "lon": left}),
        copy(5, 0, RIGHT, 3, {"lat": above, "lon": left}),
    ]
    to_bands = [
        copy(6, 1, BAND, 0, {"lat": below}),
        copy(7, 3, BAND, 1, {"lat": below}),
        copy(8, 0, BAND, 2, {"lat": above}),
        copy(9, 2, BAND, 3, {"lat": above}),
    ]

    loads[1].wait()
    weigh(1)

    def greet_and_send(sends):
        pl.semaphore_wait(barrier, len(greeted))
        for send in sends:
            send.start()

    odd = lax.rem(lon, 2) == 1

    @pl.when(odd)
    def _():
        greet_and_send(to_right)

    weigh(0)

    for load in loads[2:7]:
        load.wait()

    def make_terms(n, carry):
        at = pl.ds(pl.multiple_of(n * tile, tile), tile)
        level = lax.broadcasted_iota(jnp.int32, (depth, tile), 0) + lev * depth
        slot = lax.broadcasted_iota(jnp.int32, (depth, tile), 1) + n * tile
        away = jnp.abs(obs_level[:, at] - level).astype(jnp.float32)
        live = (slot < obs_count[0, 0]).astype(jnp.float32)
        vertical = vertical_taper(away, depth) * live
        pert = obs_pert[:, at].astype(jnp.float32)
        for m in range(depth):
            terms[m * members : (m + 1) * members, at] = (pert * vertical[m : m + 1]).astype(
                jnp.bfloat16
            )
        return carry

    lax.fori_loop(0, slots // tile, make_terms, 0)

    @pl.when(odd)
    def _():
        for send in to_bands + to_left:
            send.start()

    def offset_x(at, side):
        centre = (lax.broadcasted_iota(jnp.int32, (HALF, tile), 0) + side * HALF).astype(jnp.float32)
        return (obs_lon[:, at] - (centre + (0.5 - HALF))) * (2.0 / HALF)

    def make_rho(n, carry):
        at = pl.ds(pl.multiple_of(n * tile, tile), tile)
        squares = []
        for side in range(2):
            dx = offset_x(at, side)
            dx = jnp.where(dx < 2.0, dx, dx - 4.0)
            squares.append(dx * dx + 1e-30)
        for j in range(2 * HALF):
            dy = (obs_lat[:, at] - (j + 0.5 - HALF)) * (2.0 / HALF)
            near = dy < 2.0
            dy = jnp.where(near, dy, dy - 4.0)
            dy2 = jnp.broadcast_to(dy * dy, (HALF, tile))
            near = jnp.broadcast_to(jnp.where(near, 1.0, 0.0), (HALF, tile)) > 0.5
            for side in range(2):
                value = taper_of_square(dy2 + squares[side])
                cols = slice(side * HALF, (side + 1) * HALF)
                rho[0, j, cols, at] = jnp.where(near, value, 0.0)
                rho[1, j, cols, at] = jnp.where(near, 0.0, value)
        return carry

    lax.fori_loop(0, slots // tile, make_rho, 0)

    total[...] = jnp.zeros_like(total)

    def add_piece(piece, start, quads):
        for n in range(slots // tile):
            at = slice(n * tile, (n + 1) * tile)
            near = [offset_x(at, side) < 2.0 for side in range(2)]
            weights = cells[piece, start : start + len(quads)].reshape(len(quads) * QUAD, width)
            both = jnp.dot(weights, terms[:, at], preferred_element_type=jnp.float32)
            acc = total[:, at]
            for n_quad, (row, col) in enumerate(quads):
                a, j, b, i = row // 2, row % 2, col // 2, col % 2
                part = both[n_quad * QUAD : (n_quad + 1) * QUAD].reshape(HALF, HALF, tile)
                part = part * rho[a, j * HALF : (j + 1) * HALF, i * HALF : (i + 1) * HALF, at]
                part = jnp.sum(part, axis=0)
                keep = near[i] if b == 0 else jnp.logical_not(near[i])
                if row == 0:
                    keep = jnp.logical_and(keep, lat > 0)
                elif row == 3:
                    keep = jnp.logical_and(keep, lat < lats - 1)
                acc = acc + jnp.where(keep, part, 0.0)
            total[:, at] = acc

    add_piece(OWN, 0, [(1, 1), (2, 1), (1, 2), (2, 2)])

    @pl.when(jnp.logical_not(odd))
    def _():
        greet_and_send(to_bands + to_right + to_left)

    for send in to_left:
        send.wait_recv()
    add_piece(RIGHT, 0, [(1, 3), (2, 3), (0, 3), (3, 3)])
    for send in to_bands:
        send.wait_recv()
    add_piece(BAND, 0, [(0, 1), (0, 2), (3, 1), (3, 2)])
    to_right[0].wait_recv()
    add_piece(LEFT, 0, [(1, 0), (2, 0)])
    for send in to_right[1:]:
        send.wait_recv()
    add_piece(LEFT, 2, [(0, 0), (3, 0)])

    parts[lev] = jnp.sum(total[...], axis=0, keepdims=True)
    swaps = []
    for k in range(1, levs):
        swaps.append(
            pltpu.make_async_remote_copy(
                src_ref=parts.at[lev],
                dst_ref=parts.at[lev],
                send_sem=lev_send.at[k - 1],
                recv_sem=lev_recv.at[k - 1],
                device_id={"lev": wrapped(lev + k, levs)},
                device_id_type=MESH,
            )
        )
        swaps[-1].start()
    for swap in swaps:
        swap.wait_recv()
    value = parts[0]
    for k in range(1, levs):
        value = value + parts[k]
    for load in loads[7:]:
        load.wait()
    impact[...] = innovation[...] * inv_error[...] * value / (members - 1.0)

    for send in swaps + to_right + to_bands + to_left:
        send.wait_send()


def per_device(
    sizes,
    anomalies,
    error_grad,
    obs_lat,
    obs_lon,
    obs_level,
    obs_count,
    obs_pert,
    innovation,
    inv_error,
):
    rows, cols, width = anomalies.shape
    depth = error_grad.shape[2]
    members, slots = obs_pert.shape[2:]
    in_specs = [pl.BlockSpec(memory_space=pltpu.HBM)] * 9
    flat = (1, slots)
    impact = pl.pallas_call(
        functools.partial(kernel, sizes),
        out_shape=pltpu.VMEM(flat, jnp.float32),
        in_specs=in_specs,
        out_specs=pl.BlockSpec(memory_space=pltpu.VMEM),
        scratch_shapes=[
            pltpu.VMEM((rows, cols, width), jnp.bfloat16),
            pltpu.VMEM((rows, depth, cols), jnp.float32),
            pltpu.VMEM(flat, jnp.float32),
            pltpu.VMEM(flat, jnp.float32),
            pltpu.VMEM(flat, jnp.int32),
            pltpu.SMEM((1, 1), jnp.int32),
            pltpu.VMEM((members, slots), jnp.bfloat16),
            pltpu.VMEM(flat, jnp.float32),
            pltpu.VMEM(flat, jnp.float32),
            pltpu.VMEM((4, 4, QUAD, width), jnp.bfloat16),
            pltpu.VMEM((width, slots), jnp.bfloat16),
            pltpu.VMEM((2, rows, cols, slots), jnp.float32),
            pltpu.VMEM((HALF, slots), jnp.float32),
            pltpu.VMEM((sizes[0], 1, slots), jnp.float32),
            pltpu.SemaphoreType.DMA((9,)),
            pltpu.SemaphoreType.DMA((10,)),
            pltpu.SemaphoreType.DMA((10,)),
            pltpu.SemaphoreType.DMA((sizes[0] - 1,)),
            pltpu.SemaphoreType.DMA((sizes[0] - 1,)),
        ],
        compiler_params=pltpu.CompilerParams(
            collective_id=0, has_side_effects=True, vmem_limit_bytes=58 * 1024 * 1024
        ),
        cost_estimate=pl.CostEstimate(
            flops=2 * 4 * rows * cols * width * slots, bytes_accessed=4 * 10**6, transcendentals=0
        ),
    )(
        anomalies,
        error_grad.transpose(0, 2, 1),
        obs_lat.reshape(flat),
        obs_lon.reshape(flat),
        obs_level.reshape(flat),
        obs_count,
        obs_pert.reshape(members, slots),
        innovation.reshape(flat),
        inv_error.reshape(flat),
    )
    return impact.reshape(1, 1, slots)


def solution(mesh):
    sizes = tuple(mesh.shape[a] for a in ("lev", "lat", "lon"))
    tiles = P("lat", "lon", None)
    placed = (
        P("lat", "lon", "lev"),
        P("lat", "lon", "lev"),
        tiles,
        tiles,
        tiles,
        P("lat", "lon"),
        P("lat", "lon", None, None),
        tiles,
        tiles,
    )
    return jax.shard_map(
        functools.partial(per_device, sizes),
        mesh=mesh,
        in_specs=placed,
        out_specs=tiles,
        check_vma=False,
    )
```

```python
import functools

import jax
import jax.numpy as jnp
from jax import lax
from jax.experimental import pallas as pl
from jax.experimental.pallas import tpu as pltpu
from jax.sharding import PartitionSpec as P

MESH = pl.DeviceIdType.MESH
LANES = 128
HALF = 8
QUAD = HALF * HALF
OWN, BAND, RIGHT, LEFT = range(4)


def vertical_taper(dist, support):
    r = 2.0 * dist / support
    inner = (((-0.25 * r + 0.5) * r + 0.625) * r - 5.0 / 3.0) * r * r + 1.0
    safe_r = jnp.maximum(r, 1.0)
    outer = (
        ((((r / 12.0 - 0.5) * r + 0.625) * r + 5.0 / 3.0) * r - 5.0) * r
        + 4.0
        - 2.0 / (3.0 * safe_r)
    )
    return jnp.where(r <= 1.0, inner, jnp.where(r < 2.0, outer, 0.0))


def taper_of_square(q):
    s = lax.rsqrt(q)
    r = q * s
    inner = 1.0 + q * (0.5 * q - 5.0 / 3.0) + (q * r) * (0.625 - 0.25 * q)
    t = jnp.maximum(2.0 - r, 0.0)
    t = t * t
    outer = (t * t) * ((r + 2.0) * (1.0 / 12.0) - s * (1.0 / 24.0))
    return jnp.where(r <= 1.0, inner, outer)


def wrapped(i, n):
    return lax.rem(i + n, n)


def kernel(
    sizes,
    anomalies_in,
    error_grad_in,
    obs_lat_in,
    obs_lon_in,
    obs_level_in,
    obs_count_in,
    obs_pert_in,
    innovation_in,
    inv_error_in,
    impact,
    anomalies,
    error_grad,
    obs_lat,
    obs_lon,
    obs_level,
    obs_count,
    obs_pert,
    innovation,
    inv_error,
    cells,
    terms,
    rho,
    total,
    parts,
    in_sem,
    send_sem,
    recv_sem,
    lev_send,
    lev_recv,
    left_in,
):
    levs, lats, lons = sizes
    rows, depth, cols = error_grad.shape
    width = cells.shape[3]
    members = width // depth
    slots = terms.shape[1]
    tile = min(256, slots)
    lev, lat, lon = (lax.axis_index(a) for a in ("lev", "lat", "lon"))
    below, above = wrapped(lat + 1, lats), wrapped(lat - 1, lats)
    right, left = wrapped(lon + 1, lons), wrapped(lon - 1, lons)

    loads = [
        pltpu.make_async_copy(src, dst, in_sem.at[n])
        for n, (src, dst) in enumerate(
            (
                (error_grad_in, error_grad),
                (anomalies_in, anomalies),
                (obs_level_in, obs_level),
                (obs_count_in, obs_count),
                (obs_pert_in, obs_pert),
                (obs_lat_in, obs_lat),
                (obs_lon_in, obs_lon),
                (innovation_in, innovation),
                (inv_error_in, inv_error),
            )
        )
    ]
    for load in loads:
        load.start()

    has_above, has_below = lat > 0, lat < lats - 1

    def guarded(wanted, act):
        if wanted is None:
            act()
        else:
            pl.when(wanted)(act)

    def signal(sem, other, wanted=None):
        guarded(
            wanted,
            lambda: pl.semaphore_signal(sem, inc=1, device_id=other, device_id_type=MESH),
        )

    barrier = pltpu.get_barrier_semaphore()
    signal(barrier, {"lon": left})
    for k in range(1, levs):
        signal(barrier, {"lev": wrapped(lev + k, levs)})
    for other, wanted in ((above, has_above), (below, has_below)):
        signal(barrier, {"lat": other, "lon": left}, wanted)
        signal(barrier, {"lat": other}, wanted)
    beside = has_above.astype(jnp.int32) + has_below.astype(jnp.int32)

    pairs = rows * depth
    level_of = lax.broadcasted_iota(jnp.int32, (pairs, width), 0) % depth * members
    lane = lax.broadcasted_iota(jnp.int32, (pairs, width), 1)
    inside = jnp.logical_and(lane >= level_of, lane < level_of + members)
    ones = jnp.where(inside, 1.0, 0.0).astype(jnp.bfloat16)
    ones = jnp.concatenate([ones] * 3, axis=0)
    row_of = lax.broadcasted_iota(jnp.int32, (HALF, pairs), 1) // depth
    loads[0].wait()
    rest = error_grad[...].reshape(pairs, cols).T
    grads = []
    for _ in range(3):
        grads.append(rest.astype(jnp.bfloat16).astype(jnp.float32))
        rest = rest - grads[-1]

    def weigh(qx):
        half = slice(qx * HALF, (qx + 1) * HALF)
        wide = [
            jnp.concatenate([jnp.where(row_of == y, grad[half], 0.0) for y in range(rows)], axis=0)
            for grad in grads
        ]
        wide = jnp.concatenate(wide, axis=1).astype(jnp.bfloat16)
        spread = jnp.dot(wide, ones, preferred_element_type=jnp.float32)
        for y in range(0, rows, 2):
            both = [anomalies[n].astype(jnp.float32)[half] for n in (y, y + 1)]
            both = jnp.concatenate(both, axis=0) * spread[y * HALF : (y + 2) * HALF]
            at = y % HALF * HALF
            cells[OWN, qx * 2 + y // HALF, at : at + 2 * HALF] = both.astype(jnp.bfloat16)

    class Copy:
        def __init__(self, sem, quads, piece, place, device, sends=None, gets=None):
            self.sends, self.gets = sends, gets
            self.copy = pltpu.make_async_remote_copy(
                src_ref=cells.at[OWN, quads],
                dst_ref=cells.at[piece, place],
                send_sem=send_sem.at[sem],
                recv_sem=recv_sem.at[sem],
                device_id=device,
                device_id_type=MESH,
            )

        def start(self):
            guarded(self.sends, self.copy.start)

        def wait_recv(self):
            guarded(self.gets, self.copy.wait_recv)

        def wait_send(self):
            guarded(self.sends, self.copy.wait_send)

    down, up = (has_below, has_above), (has_above, has_below)
    to_right = [
        Copy(1, 3, LEFT, 2, {"lat": below, "lon": right}, *down),
        Copy(2, 2, LEFT, 3, {"lat": above, "lon": right}, *up),
        Copy(0, pl.ds(2, 2), LEFT, pl.ds(0, 2), {"lon": right}),
    ]
    to_left = [
        Copy(4, 1, RIGHT, 2, {"lat": below, "lon": left}, *down),
        Copy(5, 0, RIGHT, 3, {"lat": above, "lon": left}, *up),
        Copy(3, pl.ds(0, 2), RIGHT, pl.ds(0, 2), {"lon": left}),
    ]
    to_bands = [
        Copy(6, 1, BAND, 0, {"lat": below}, *down),
        Copy(7, 3, BAND, 1, {"lat": below}, *down),
        Copy(8, 0, BAND, 2, {"lat": above}, *up),
        Copy(9, 2, BAND, 3, {"lat": above}, *up),
    ]

    loads[1].wait()
    weigh(1)
    pl.semaphore_wait(barrier, levs + 2 * beside)
    for send in to_right:
        send.start()
    signal(left_in, {"lon": right})
    for other, wanted in ((above, has_above), (below, has_below)):
        signal(left_in, {"lat": other, "lon": right}, wanted)
    weigh(0)
    for send in to_bands:
        send.start()

    for load in loads[2:7]:
        load.wait()

    def make_terms(n, carry):
        at = pl.ds(pl.multiple_of(n * tile, tile), tile)
        level = lax.broadcasted_iota(jnp.int32, (depth, tile), 0) + lev * depth
        slot = lax.broadcasted_iota(jnp.int32, (depth, tile), 1) + n * tile
        away = jnp.abs(obs_level[:, at] - level).astype(jnp.float32)
        live = (slot < obs_count[0, 0]).astype(jnp.float32)
        vertical = vertical_taper(away, depth) * live
        pert = obs_pert[:, at].astype(jnp.float32)
        for m in range(depth):
            terms[m * members : (m + 1) * members, at] = (pert * vertical[m : m + 1]).astype(
                jnp.bfloat16
            )
        return carry

    lax.fori_loop(0, slots // tile, make_terms, 0)

    def offset_x(at, side):
        centre = (lax.broadcasted_iota(jnp.int32, (HALF, tile), 0) + side * HALF).astype(jnp.float32)
        return (obs_lon[:, at] - (centre + (0.5 - HALF))) * (2.0 / HALF)

    def make_rho(n, carry):
        at = pl.ds(pl.multiple_of(n * tile, tile), tile)
        squares = []
        for side in range(2):
            dx = offset_x(at, side)
            dx = jnp.where(dx < 2.0, dx, dx - 4.0)
            squares.append(dx * dx + 1e-30)
        for j in range(2 * HALF):
            dy = (obs_lat[:, at] - (j + 0.5 - HALF)) * (2.0 / HALF)
            near = dy < 2.0
            dy = jnp.where(near, dy, dy - 4.0)
            dy2 = jnp.broadcast_to(dy * dy, (HALF, tile))
            near = jnp.broadcast_to(jnp.where(near, 1.0, 0.0), (HALF, tile)) > 0.5
            for side in range(2):
                value = taper_of_square(dy2 + squares[side])
                cols = slice(side * HALF, (side + 1) * HALF)
                rho[0, j, cols, at] = jnp.where(near, value, 0.0)
                rho[1, j, cols, at] = jnp.where(near, 0.0, value)
        return carry

    lax.fori_loop(0, slots // tile, make_rho, 0)

    def send_left():
        pl.semaphore_wait(left_in, 1 + beside)
        for send in to_left:
            send.start()

    @pl.when(lon > 0)
    def _():
        send_left()

    total[...] = jnp.zeros_like(total)

    def add_piece(piece, start, quads):
        for n in range(slots // tile):
            at = slice(n * tile, (n + 1) * tile)
            near = [offset_x(at, side) < 2.0 for side in range(2)]
            weights = cells[piece, start : start + len(quads)].reshape(len(quads) * QUAD, width)
            both = jnp.dot(weights, terms[:, at], preferred_element_type=jnp.float32)
            acc = total[:, at]
            for n_quad, (row, col) in enumerate(quads):
                a, j, b, i = row // 2, row % 2, col // 2, col % 2
                part = both[n_quad * QUAD : (n_quad + 1) * QUAD].reshape(HALF, HALF, tile)
                part = part * rho[a, j * HALF : (j + 1) * HALF, i * HALF : (i + 1) * HALF, at]
                part = jnp.sum(part, axis=0)
                keep = near[i] if b == 0 else jnp.logical_not(near[i])
                if row == 0:
                    keep = jnp.logical_and(keep, lat > 0)
                elif row == 3:
                    keep = jnp.logical_and(keep, lat < lats - 1)
                acc = acc + jnp.where(keep, part, 0.0)
            total[:, at] = acc

    add_piece(OWN, 0, [(1, 1), (2, 1), (1, 2), (2, 2)])

    for send in to_bands:
        send.wait_recv()
    add_piece(BAND, 0, [(0, 1), (0, 2), (3, 1), (3, 2)])
    @pl.when(lon == 0)
    def _():
        send_left()

    for send in to_left:
        send.wait_recv()
    add_piece(RIGHT, 0, [(1, 3), (2, 3), (0, 3), (3, 3)])
    for send in to_right[:2]:
        send.wait_recv()
    add_piece(LEFT, 2, [(0, 0), (3, 0)])
    to_right[2].wait_recv()
    add_piece(LEFT, 0, [(1, 0), (2, 0)])

    parts[lev] = jnp.sum(total[...], axis=0, keepdims=True)
    swaps = []
    for k in range(1, levs):
        swaps.append(
            pltpu.make_async_remote_copy(
                src_ref=parts.at[lev],
                dst_ref=parts.at[lev],
                send_sem=lev_send.at[k - 1],
                recv_sem=lev_recv.at[k - 1],
                device_id={"lev": wrapped(lev + k, levs)},
                device_id_type=MESH,
            )
        )
        swaps[-1].start()
    for swap in swaps:
        swap.wait_recv()
    value = parts[0]
    for k in range(1, levs):
        value = value + parts[k]
    for load in loads[7:]:
        load.wait()
    impact[...] = innovation[...] * inv_error[...] * value / (members - 1.0)

    for send in swaps + to_right + to_bands + to_left:
        send.wait_send()


def per_device(
    sizes,
    anomalies,
    error_grad,
    obs_lat,
    obs_lon,
    obs_level,
    obs_count,
    obs_pert,
    innovation,
    inv_error,
):
    rows, cols, width = anomalies.shape
    depth = error_grad.shape[2]
    members, slots = obs_pert.shape[2:]
    in_specs = [pl.BlockSpec(memory_space=pltpu.HBM)] * 9
    flat = (1, slots)
    impact = pl.pallas_call(
        functools.partial(kernel, sizes),
        out_shape=pltpu.VMEM(flat, jnp.float32),
        in_specs=in_specs,
        out_specs=pl.BlockSpec(memory_space=pltpu.VMEM),
        scratch_shapes=[
            pltpu.VMEM((rows, cols, width), jnp.bfloat16),
            pltpu.VMEM((rows, depth, cols), jnp.float32),
            pltpu.VMEM(flat, jnp.float32),
            pltpu.VMEM(flat, jnp.float32),
            pltpu.VMEM(flat, jnp.int32),
            pltpu.SMEM((1, 1), jnp.int32),
            pltpu.VMEM((members, slots), jnp.bfloat16),
            pltpu.VMEM(flat, jnp.float32),
            pltpu.VMEM(flat, jnp.float32),
            pltpu.VMEM((4, 4, QUAD, width), jnp.bfloat16),
            pltpu.VMEM((width, slots), jnp.bfloat16),
            pltpu.VMEM((2, rows, cols, slots), jnp.float32),
            pltpu.VMEM((HALF, slots), jnp.float32),
            pltpu.VMEM((sizes[0], 1, slots), jnp.float32),
            pltpu.SemaphoreType.DMA((9,)),
            pltpu.SemaphoreType.DMA((10,)),
            pltpu.SemaphoreType.DMA((10,)),
            pltpu.SemaphoreType.DMA((sizes[0] - 1,)),
            pltpu.SemaphoreType.DMA((sizes[0] - 1,)),
            pltpu.SemaphoreType.REGULAR,
        ],
        compiler_params=pltpu.CompilerParams(
            collective_id=0, has_side_effects=True, vmem_limit_bytes=58 * 1024 * 1024
        ),
        cost_estimate=pl.CostEstimate(
            flops=2 * 4 * rows * cols * width * slots, bytes_accessed=4 * 10**6, transcendentals=0
        ),
    )(
        anomalies,
        error_grad.transpose(0, 2, 1),
        obs_lat.reshape(flat),
        obs_lon.reshape(flat),
        obs_level.reshape(flat),
        obs_count,
        obs_pert.reshape(members, slots),
        innovation.reshape(flat),
        inv_error.reshape(flat),
    )
    return impact.reshape(1, 1, slots)


def solution(mesh):
    sizes = tuple(mesh.shape[a] for a in ("lev", "lat", "lon"))
    tiles = P("lat", "lon", None)
    placed = (
        P("lat", "lon", "lev"),
        P("lat", "lon", "lev"),
        tiles,
        tiles,
        tiles,
        P("lat", "lon"),
        P("lat", "lon", None, None),
        tiles,
        tiles,
    )
    return jax.shard_map(
        functools.partial(per_device, sizes),
        mesh=mesh,
        in_specs=placed,
        out_specs=tiles,
        check_vma=False,
    )
```

```python
import functools

import jax
import jax.numpy as jnp
from jax import lax
from jax.experimental import pallas as pl
from jax.experimental.pallas import tpu as pltpu
from jax.sharding import PartitionSpec as P

MESH = pl.DeviceIdType.MESH
LANES = 128
HALF = 8
QUAD = HALF * HALF
OWN, BAND, RIGHT, LEFT = range(4)


def vertical_taper(dist, support):
    r = 2.0 * dist / support
    inner = (((-0.25 * r + 0.5) * r + 0.625) * r - 5.0 / 3.0) * r * r + 1.0
    safe_r = jnp.maximum(r, 1.0)
    outer = (
        ((((r / 12.0 - 0.5) * r + 0.625) * r + 5.0 / 3.0) * r - 5.0) * r
        + 4.0
        - 2.0 / (3.0 * safe_r)
    )
    return jnp.where(r <= 1.0, inner, jnp.where(r < 2.0, outer, 0.0))


def taper_of_square(q):
    s = lax.rsqrt(q)
    r = q * s
    inner = 1.0 + q * (0.5 * q - 5.0 / 3.0) + (q * r) * (0.625 - 0.25 * q)
    t = jnp.maximum(2.0 - r, 0.0)
    t = t * t
    outer = (t * t) * ((r + 2.0) * (1.0 / 12.0) - s * (1.0 / 24.0))
    return jnp.where(r <= 1.0, inner, outer)


def wrapped(i, n):
    return lax.rem(i + n, n)


def kernel(
    sizes,
    anomalies_in,
    error_grad_in,
    obs_lat_in,
    obs_lon_in,
    obs_level_in,
    obs_count_in,
    obs_pert_in,
    innovation_in,
    inv_error_in,
    impact,
    anomalies,
    error_grad,
    obs_lat,
    obs_lon,
    obs_level,
    obs_count,
    obs_pert,
    innovation,
    inv_error,
    cells,
    terms,
    rho,
    total,
    parts,
    in_sem,
    send_sem,
    recv_sem,
    lev_send,
    lev_recv,
    left_in,
    levs_in,
):
    levs, lats, lons = sizes
    rows, depth, cols = error_grad.shape
    width = cells.shape[3]
    members = width // depth
    slots = terms.shape[1]
    tile = min(256, slots)
    lev, lat, lon = (lax.axis_index(a) for a in ("lev", "lat", "lon"))
    below, above = wrapped(lat + 1, lats), wrapped(lat - 1, lats)
    right, left = wrapped(lon + 1, lons), wrapped(lon - 1, lons)

    has_above, has_below = lat > 0, lat < lats - 1

    def guarded(wanted, act):
        if wanted is None:
            act()
        else:
            pl.when(wanted)(act)

    def signal(sem, other, wanted=None):
        guarded(
            wanted,
            lambda: pl.semaphore_signal(sem, inc=1, device_id=other, device_id_type=MESH),
        )

    leads = lev == 0
    barrier = pltpu.get_barrier_semaphore()
    signal(barrier, {"lev": 0}, jnp.logical_not(leads))
    for other, wanted in ((above, has_above), (below, has_below)):
        signal(barrier, {"lat": other}, wanted)

    loads = [
        pltpu.make_async_copy(src, dst, in_sem.at[n])
        for n, (src, dst) in enumerate(
            (
                (error_grad_in, error_grad),
                (anomalies_in, anomalies),
                (obs_level_in, obs_level),
                (obs_count_in, obs_count),
                (obs_pert_in, obs_pert),
                (obs_lat_in, obs_lat),
                (obs_lon_in, obs_lon),
                (innovation_in, innovation),
                (inv_error_in, inv_error),
            )
        )
    ]
    for load in loads[:2]:
        load.start()
    signal(barrier, {"lon": left})
    for other, wanted in ((above, has_above), (below, has_below)):
        signal(barrier, {"lat": other, "lon": left}, wanted)
    for load in loads[2:]:
        load.start()

    beside = has_above.astype(jnp.int32) + has_below.astype(jnp.int32)

    pairs = rows * depth
    level_of = lax.broadcasted_iota(jnp.int32, (pairs, width), 0) % depth * members
    lane = lax.broadcasted_iota(jnp.int32, (pairs, width), 1)
    inside = jnp.logical_and(lane >= level_of, lane < level_of + members)
    ones = jnp.where(inside, 1.0, 0.0).astype(jnp.bfloat16)
    ones = jnp.concatenate([ones] * 3, axis=0)
    row_of = lax.broadcasted_iota(jnp.int32, (HALF, pairs), 1) // depth
    loads[0].wait()
    rest = error_grad[...].reshape(pairs, cols).T
    grads = []
    for _ in range(3):
        grads.append(rest.astype(jnp.bfloat16).astype(jnp.float32))
        rest = rest - grads[-1]

    def weigh(qx):
        half = slice(qx * HALF, (qx + 1) * HALF)
        wide = [
            jnp.concatenate([jnp.where(row_of == y, grad[half], 0.0) for y in range(rows)], axis=0)
            for grad in grads
        ]
        wide = jnp.concatenate(wide, axis=1).astype(jnp.bfloat16)
        spread = jnp.dot(wide, ones, preferred_element_type=jnp.float32)
        for y in range(0, rows, 2):
            both = [anomalies[n].astype(jnp.float32)[half] for n in (y, y + 1)]
            both = jnp.concatenate(both, axis=0) * spread[y * HALF : (y + 2) * HALF]
            at = y % HALF * HALF
            cells[OWN, qx * 2 + y // HALF, at : at + 2 * HALF] = both.astype(jnp.bfloat16)

    class Copy:
        def __init__(self, sem, quads, piece, place, device, sends=None, gets=None):
            self.sends, self.gets = sends, gets
            self.copy = pltpu.make_async_remote_copy(
                src_ref=cells.at[OWN, quads],
                dst_ref=cells.at[piece, place],
                send_sem=send_sem.at[sem],
                recv_sem=recv_sem.at[sem],
                device_id=device,
                device_id_type=MESH,
            )

        def start(self):
            guarded(self.sends, self.copy.start)

        def wait_recv(self):
            guarded(self.gets, self.copy.wait_recv)

        def wait_send(self):
            guarded(self.sends, self.copy.wait_send)

    down, up = (has_below, has_above), (has_above, has_below)
    to_right = [
        Copy(1, 3, LEFT, 2, {"lat": below, "lon": right}, *down),
        Copy(2, 2, LEFT, 3, {"lat": above, "lon": right}, *up),
        Copy(0, pl.ds(2, 2), LEFT, pl.ds(0, 2), {"lon": right}),
    ]
    to_left = [
        Copy(4, 1, RIGHT, 2, {"lat": below, "lon": left}, *down),
        Copy(5, 0, RIGHT, 3, {"lat": above, "lon": left}, *up),
        Copy(3, pl.ds(0, 2), RIGHT, pl.ds(0, 2), {"lon": left}),
    ]
    to_bands = [
        Copy(6, 1, BAND, 0, {"lat": below}, *down),
        Copy(7, 3, BAND, 1, {"lat": below}, *down),
        Copy(8, 0, BAND, 2, {"lat": above}, *up),
        Copy(9, 2, BAND, 3, {"lat": above}, *up),
    ]

    loads[1].wait()
    weigh(1)
    pl.semaphore_wait(barrier, 1 + 2 * beside + jnp.where(leads, levs - 1, 0))
    for send in to_right:
        send.start()

    @pl.when(leads)
    def _():
        for k in range(1, levs):
            signal(levs_in, {"lev": k})

    signal(left_in, {"lon": right})
    for other, wanted in ((above, has_above), (below, has_below)):
        signal(left_in, {"lat": other, "lon": right}, wanted)
    weigh(0)
    for send in to_bands:
        send.start()

    for load in loads[2:7]:
        load.wait()

    def make_terms(n, carry):
        at = pl.ds(pl.multiple_of(n * tile, tile), tile)
        level = lax.broadcasted_iota(jnp.int32, (depth, tile), 0) + lev * depth
        slot = lax.broadcasted_iota(jnp.int32, (depth, tile), 1) + n * tile
        away = jnp.abs(obs_level[:, at] - level).astype(jnp.float32)
        live = (slot < obs_count[0, 0]).astype(jnp.float32)
        vertical = vertical_taper(away, depth) * live
        pert = obs_pert[:, at].astype(jnp.float32)
        for m in range(depth):
            terms[m * members : (m + 1) * members, at] = (pert * vertical[m : m + 1]).astype(
                jnp.bfloat16
            )
        return carry

    lax.fori_loop(0, slots // tile, make_terms, 0)

    def offset_x(at, side):
        centre = (lax.broadcasted_iota(jnp.int32, (HALF, tile), 0) + side * HALF).astype(jnp.float32)
        return (obs_lon[:, at] - (centre + (0.5 - HALF))) * (2.0 / HALF)

    def make_rho(n, carry):
        at = pl.ds(pl.multiple_of(n * tile, tile), tile)
        squares = []
        for side in range(2):
            dx = offset_x(at, side)
            dx = jnp.where(dx < 2.0, dx, dx - 4.0)
            squares.append(dx * dx + 1e-30)
        for j in range(2 * HALF):
            dy = (obs_lat[:, at] - (j + 0.5 - HALF)) * (2.0 / HALF)
            near = dy < 2.0
            dy = jnp.where(near, dy, dy - 4.0)
            dy2 = jnp.broadcast_to(dy * dy, (HALF, tile))
            near = jnp.broadcast_to(jnp.where(near, 1.0, 0.0), (HALF, tile)) > 0.5
            for side in range(2):
                value = taper_of_square(dy2 + squares[side])
                cols = slice(side * HALF, (side + 1) * HALF)
                rho[0, j, cols, at] = jnp.where(near, value, 0.0)
                rho[1, j, cols, at] = jnp.where(near, 0.0, value)
        return carry

    lax.fori_loop(0, slots // tile, make_rho, 0)

    def send_left():
        pl.semaphore_wait(left_in, 1 + beside)
        for send in to_left:
            send.start()

    @pl.when(lon > 0)
    def _():
        send_left()

    total[...] = jnp.zeros_like(total)

    def add_piece(piece, start, quads):
        for n in range(slots // tile):
            at = slice(n * tile, (n + 1) * tile)
            near = [offset_x(at, side) < 2.0 for side in range(2)]
            weights = cells[piece, start : start + len(quads)].reshape(len(quads) * QUAD, width)
            both = jnp.dot(weights, terms[:, at], preferred_element_type=jnp.float32)
            acc = total[:, at]
            for n_quad, (row, col) in enumerate(quads):
                a, j, b, i = row // 2, row % 2, col // 2, col % 2
                part = both[n_quad * QUAD : (n_quad + 1) * QUAD].reshape(HALF, HALF, tile)
                part = part * rho[a, j * HALF : (j + 1) * HALF, i * HALF : (i + 1) * HALF, at]
                part = jnp.sum(part, axis=0)
                keep = near[i] if b == 0 else jnp.logical_not(near[i])
                if row == 0:
                    keep = jnp.logical_and(keep, lat > 0)
                elif row == 3:
                    keep = jnp.logical_and(keep, lat < lats - 1)
                acc = acc + jnp.where(keep, part, 0.0)
            total[:, at] = acc

    add_piece(OWN, 0, [(1, 1), (2, 1), (1, 2), (2, 2)])

    for send in to_bands:
        send.wait_recv()
    add_piece(BAND, 0, [(0, 1), (0, 2), (3, 1), (3, 2)])
    @pl.when(lon == 0)
    def _():
        send_left()

    for send in to_left:
        send.wait_recv()
    add_piece(RIGHT, 0, [(1, 3), (2, 3), (0, 3), (3, 3)])
    for send in to_right[:2]:
        send.wait_recv()
    add_piece(LEFT, 2, [(0, 0), (3, 0)])
    to_right[2].wait_recv()
    add_piece(LEFT, 0, [(1, 0), (2, 0)])

    @pl.when(jnp.logical_not(leads))
    def _():
        pl.semaphore_wait(levs_in, 1)

    parts[lev] = jnp.sum(total[...], axis=0, keepdims=True)
    swaps = []
    for k in range(1, levs):
        swaps.append(
            pltpu.make_async_remote_copy(
                src_ref=parts.at[lev],
                dst_ref=parts.at[lev],
                send_sem=lev_send.at[k - 1],
                recv_sem=lev_recv.at[k - 1],
                device_id={"lev": wrapped(lev + k, levs)},
                device_id_type=MESH,
            )
        )
        swaps[-1].start()
    for swap in swaps:
        swap.wait_recv()
    value = parts[0]
    for k in range(1, levs):
        value = value + parts[k]
    for load in loads[7:]:
        load.wait()
    impact[...] = innovation[...] * inv_error[...] * value / (members - 1.0)

    for send in swaps + to_right + to_bands + to_left:
        send.wait_send()


def per_device(
    sizes,
    anomalies,
    error_grad,
    obs_lat,
    obs_lon,
    obs_level,
    obs_count,
    obs_pert,
    innovation,
    inv_error,
):
    rows, cols, width = anomalies.shape
    depth = error_grad.shape[2]
    members, slots = obs_pert.shape[2:]
    in_specs = [pl.BlockSpec(memory_space=pltpu.HBM)] * 9
    flat = (1, slots)
    impact = pl.pallas_call(
        functools.partial(kernel, sizes),
        out_shape=pltpu.VMEM(flat, jnp.float32),
        in_specs=in_specs,
        out_specs=pl.BlockSpec(memory_space=pltpu.VMEM),
        scratch_shapes=[
            pltpu.VMEM((rows, cols, width), jnp.bfloat16),
            pltpu.VMEM((rows, depth, cols), jnp.float32),
            pltpu.VMEM(flat, jnp.float32),
            pltpu.VMEM(flat, jnp.float32),
            pltpu.VMEM(flat, jnp.int32),
            pltpu.SMEM((1, 1), jnp.int32),
            pltpu.VMEM((members, slots), jnp.bfloat16),
            pltpu.VMEM(flat, jnp.float32),
            pltpu.VMEM(flat, jnp.float32),
            pltpu.VMEM((4, 4, QUAD, width), jnp.bfloat16),
            pltpu.VMEM((width, slots), jnp.bfloat16),
            pltpu.VMEM((2, rows, cols, slots), jnp.float32),
            pltpu.VMEM((HALF, slots), jnp.float32),
            pltpu.VMEM((sizes[0], 1, slots), jnp.float32),
            pltpu.SemaphoreType.DMA((9,)),
            pltpu.SemaphoreType.DMA((10,)),
            pltpu.SemaphoreType.DMA((10,)),
            pltpu.SemaphoreType.DMA((sizes[0] - 1,)),
            pltpu.SemaphoreType.DMA((sizes[0] - 1,)),
            pltpu.SemaphoreType.REGULAR,
            pltpu.SemaphoreType.REGULAR,
        ],
        compiler_params=pltpu.CompilerParams(
            collective_id=0, has_side_effects=True, vmem_limit_bytes=58 * 1024 * 1024
        ),
        cost_estimate=pl.CostEstimate(
            flops=2 * 4 * rows * cols * width * slots, bytes_accessed=4 * 10**6, transcendentals=0
        ),
    )(
        anomalies,
        error_grad.transpose(0, 2, 1),
        obs_lat.reshape(flat),
        obs_lon.reshape(flat),
        obs_level.reshape(flat),
        obs_count,
        obs_pert.reshape(members, slots),
        innovation.reshape(flat),
        inv_error.reshape(flat),
    )
    return impact.reshape(1, 1, slots)


def solution(mesh):
    sizes = tuple(mesh.shape[a] for a in ("lev", "lat", "lon"))
    tiles = P("lat", "lon", None)
    placed = (
        P("lat", "lon", "lev"),
        P("lat", "lon", "lev"),
        tiles,
        tiles,
        tiles,
        P("lat", "lon"),
        P("lat", "lon", None, None),
        tiles,
        tiles,
    )
    return jax.shard_map(
        functools.partial(per_device, sizes),
        mesh=mesh,
        in_specs=placed,
        out_specs=tiles,
        check_vma=False,
    )
```

```python
import functools

import jax
import jax.numpy as jnp
from jax import lax
from jax.experimental import pallas as pl
from jax.experimental.pallas import tpu as pltpu
from jax.sharding import PartitionSpec as P

MESH = pl.DeviceIdType.MESH
LANES = 128
HALF = 8
QUAD = HALF * HALF
OWN, BAND, RIGHT, LEFT = range(4)


def vertical_taper(dist, support):
    r = 2.0 * dist / support
    inner = (((-0.25 * r + 0.5) * r + 0.625) * r - 5.0 / 3.0) * r * r + 1.0
    safe_r = jnp.maximum(r, 1.0)
    outer = (
        ((((r / 12.0 - 0.5) * r + 0.625) * r + 5.0 / 3.0) * r - 5.0) * r
        + 4.0
        - 2.0 / (3.0 * safe_r)
    )
    return jnp.where(r <= 1.0, inner, jnp.where(r < 2.0, outer, 0.0))


def taper_of_square(q):
    s = lax.rsqrt(q)
    r = q * s
    inner = 1.0 + q * (0.5 * q - 5.0 / 3.0) + (q * r) * (0.625 - 0.25 * q)
    t = jnp.maximum(2.0 - r, 0.0)
    t = t * t
    outer = (t * t) * ((r + 2.0) * (1.0 / 12.0) - s * (1.0 / 24.0))
    return jnp.where(r <= 1.0, inner, outer)


def wrapped(i, n):
    return lax.rem(i + n, n)


def kernel(
    sizes,
    anomalies_in,
    error_grad_in,
    obs_lat_in,
    obs_lon_in,
    obs_level_in,
    obs_count_in,
    obs_pert_in,
    innovation_in,
    inv_error_in,
    impact,
    anomalies,
    error_grad,
    obs_lat,
    obs_lon,
    obs_level,
    obs_count,
    obs_pert,
    innovation,
    inv_error,
    cells,
    terms,
    rho,
    total,
    parts,
    in_sem,
    send_sem,
    recv_sem,
    lev_send,
    lev_recv,
    left_in,
    levs_in,
    strip_sem,
):
    levs, lats, lons = sizes
    rows, depth, cols = error_grad.shape
    width = cells.shape[3]
    members = width // depth
    slots = terms.shape[1]
    tile = min(256, slots)
    lev, lat, lon = (lax.axis_index(a) for a in ("lev", "lat", "lon"))
    below, above = wrapped(lat + 1, lats), wrapped(lat - 1, lats)
    right, left = wrapped(lon + 1, lons), wrapped(lon - 1, lons)

    loads = [
        pltpu.make_async_copy(src, dst, in_sem.at[n])
        for n, (src, dst) in enumerate(
            (
                (error_grad_in, error_grad),
                (obs_level_in, obs_level),
                (obs_count_in, obs_count),
                (obs_pert_in, obs_pert),
                (obs_lat_in, obs_lat),
                (obs_lon_in, obs_lon),
                (innovation_in, innovation),
                (inv_error_in, inv_error),
            )
        )
    ]
    share = rows // 4
    strips = [
        pltpu.make_async_copy(
            anomalies_in.at[pl.ds(n * share, share)],
            anomalies.at[pl.ds(n * share, share)],
            strip_sem.at[n],
        )
        for n in range(4)
    ]
    for load in [loads[0], *strips[2:], *strips[:2]]:
        load.start()

    has_above, has_below = lat > 0, lat < lats - 1

    def guarded(wanted, act):
        if wanted is None:
            act()
        else:
            pl.when(wanted)(act)

    def signal(sem, other, wanted=None):
        guarded(
            wanted,
            lambda: pl.semaphore_signal(sem, inc=1, device_id=other, device_id_type=MESH),
        )

    inner = lon < lons - 1
    leads = lev == 0
    barrier = pltpu.get_barrier_semaphore()
    signal(barrier, {"lev": 0}, jnp.logical_not(leads))
    for other, wanted in ((above, has_above), (below, has_below)):
        signal(barrier, {"lat": other}, jnp.logical_and(wanted, inner))

    signal(barrier, {"lon": left})
    for other, wanted in ((above, has_above), (below, has_below)):
        signal(barrier, {"lat": other, "lon": left}, wanted)

    beside = has_above.astype(jnp.int32) + has_below.astype(jnp.int32)

    pairs = rows * depth
    level_of = lax.broadcasted_iota(jnp.int32, (pairs, width), 0) % depth * members
    lane = lax.broadcasted_iota(jnp.int32, (pairs, width), 1)
    inside = jnp.logical_and(lane >= level_of, lane < level_of + members)
    ones = jnp.where(inside, 1.0, 0.0).astype(jnp.bfloat16)
    ones = jnp.concatenate([ones] * 3, axis=0)
    row_of = lax.broadcasted_iota(jnp.int32, (HALF, pairs), 1) // depth
    loads[0].wait()
    rest = error_grad[...].reshape(pairs, cols).T
    grads = []
    for _ in range(3):
        grads.append(rest.astype(jnp.bfloat16).astype(jnp.float32))
        rest = rest - grads[-1]

    def spread_over(qx):
        half = slice(qx * HALF, (qx + 1) * HALF)
        wide = [
            jnp.concatenate([jnp.where(row_of == y, grad[half], 0.0) for y in range(rows)], axis=0)
            for grad in grads
        ]
        wide = jnp.concatenate(wide, axis=1).astype(jnp.bfloat16)
        return jnp.dot(wide, ones, preferred_element_type=jnp.float32)

    def weigh(qx, qy, spread):
        half = slice(qx * HALF, (qx + 1) * HALF)
        for y in range(qy * HALF, (qy + 1) * HALF, 2):
            both = [anomalies[n].astype(jnp.float32)[half] for n in (y, y + 1)]
            both = jnp.concatenate(both, axis=0) * spread[y * HALF : (y + 2) * HALF]
            at = y % HALF * HALF
            cells[OWN, qx * 2 + y // HALF, at : at + 2 * HALF] = both.astype(jnp.bfloat16)

    class Copy:
        def __init__(
            self, sem, quads, piece, place, device, sends=None, gets=None, part=slice(None)
        ):
            self.sends, self.gets = sends, gets
            self.copy = pltpu.make_async_remote_copy(
                src_ref=cells.at[OWN, quads, :, part],
                dst_ref=cells.at[piece, place, :, part],
                send_sem=send_sem.at[sem],
                recv_sem=recv_sem.at[sem],
                device_id=device,
                device_id_type=MESH,
            )

        def start(self):
            guarded(self.sends, self.copy.start)

        def wait_recv(self):
            guarded(self.gets, self.copy.wait_recv)

        def wait_send(self):
            guarded(self.sends, self.copy.wait_send)

    down, up = (has_below, has_above), (has_above, has_below)
    to_right = [
        Copy(1, 3, LEFT, 2, {"lat": below, "lon": right}, *down),
        Copy(2, 2, LEFT, 3, {"lat": above, "lon": right}, *up),
    ]
    cut = width * 4 // 5 // LANES * LANES
    spans = [slice(0, cut), slice(cut, width)]
    to_right += [
        Copy(sem, pl.ds(2, 2), LEFT, pl.ds(0, 2), {"lon": right}, part=span)
        for sem, span in zip((0, 10), spans)
    ]
    to_left = [
        Copy(4, 1, RIGHT, 2, {"lat": below, "lon": left}, *down),
        Copy(5, 0, RIGHT, 3, {"lat": above, "lon": left}, *up),
        Copy(3, pl.ds(0, 2), RIGHT, pl.ds(0, 2), {"lon": left}),
    ]
    to_bands = [
        Copy(6, 1, BAND, 0, {"lat": below}, *down),
        Copy(7, 3, BAND, 1, {"lat": below}, *down),
        Copy(8, 0, BAND, 2, {"lat": above}, *up),
        Copy(9, 2, BAND, 3, {"lat": above}, *up),
    ]

    spread = spread_over(1)
    for strip in strips[2:]:
        strip.wait()
    weigh(1, 1, spread)
    bands_in = jnp.where(inner, beside, 0)
    pl.semaphore_wait(barrier, 1 + beside + bands_in + jnp.where(leads, levs - 1, 0))
    to_right[0].start()
    for strip in strips[:2]:
        strip.wait()
    weigh(1, 0, spread)
    for send in to_right[1:]:
        send.start()
    for load in loads[1:]:
        load.start()

    @pl.when(leads)
    def _():
        for k in range(1, levs):
            signal(levs_in, {"lev": k})

    signal(left_in, {"lon": right})
    for other, wanted in ((above, has_above), (below, has_below)):
        signal(left_in, {"lat": other, "lon": right}, wanted)
    spread = spread_over(0)
    for qy in range(2):
        weigh(0, qy, spread)

    def send_bands():
        for send in to_bands:
            send.start()

    pl.when(inner)(send_bands)

    for load in loads[1:6]:
        load.wait()

    def make_terms(n, carry):
        at = pl.ds(pl.multiple_of(n * tile, tile), tile)
        level = lax.broadcasted_iota(jnp.int32, (depth, tile), 0) + lev * depth
        slot = lax.broadcasted_iota(jnp.int32, (depth, tile), 1) + n * tile
        away = jnp.abs(obs_level[:, at] - level).astype(jnp.float32)
        live = (slot < obs_count[0, 0]).astype(jnp.float32)
        vertical = vertical_taper(away, depth) * live
        pert = obs_pert[:, at].astype(jnp.float32)
        for m in range(depth):
            terms[m * members : (m + 1) * members, at] = (pert * vertical[m : m + 1]).astype(
                jnp.bfloat16
            )
        return carry

    lax.fori_loop(0, slots // tile, make_terms, 0)

    def offset_x(at, side):
        centre = (lax.broadcasted_iota(jnp.int32, (HALF, tile), 0) + side * HALF).astype(jnp.float32)
        return (obs_lon[:, at] - (centre + (0.5 - HALF))) * (2.0 / HALF)

    def make_rho(n, carry):
        at = pl.ds(pl.multiple_of(n * tile, tile), tile)
        squares = []
        for side in range(2):
            dx = offset_x(at, side)
            dx = jnp.where(dx < 2.0, dx, dx - 4.0)
            squares.append(dx * dx + 1e-30)
        for j in range(2 * HALF):
            dy = (obs_lat[:, at] - (j + 0.5 - HALF)) * (2.0 / HALF)
            near = dy < 2.0
            dy = jnp.where(near, dy, dy - 4.0)
            dy2 = jnp.broadcast_to(dy * dy, (HALF, tile))
            near = jnp.broadcast_to(jnp.where(near, 1.0, 0.0), (HALF, tile)) > 0.5
            for side in range(2):
                value = taper_of_square(dy2 + squares[side])
                cols = slice(side * HALF, (side + 1) * HALF)
                rho[0, j, cols, at] = jnp.where(near, value, 0.0)
                rho[1, j, cols, at] = jnp.where(near, 0.0, value)
        return carry

    lax.fori_loop(0, slots // tile, make_rho, 0)

    def send_left():
        pl.semaphore_wait(left_in, 1 + beside)
        for send in to_left:
            send.start()

    @pl.when(lon > 0)
    def _():
        send_left()

    pl.when(jnp.logical_not(inner))(send_bands)

    total[...] = jnp.zeros_like(total)

    def add_piece(piece, start, quads, span=slice(None)):
        for n in range(slots // tile):
            at = slice(n * tile, (n + 1) * tile)
            near = [offset_x(at, side) < 2.0 for side in range(2)]
            weights = cells[piece, start : start + len(quads), :, span].reshape(len(quads) * QUAD, -1)
            both = jnp.dot(weights, terms[span, at], preferred_element_type=jnp.float32)
            acc = total[:, at]
            for n_quad, (row, col) in enumerate(quads):
                a, j, b, i = row // 2, row % 2, col // 2, col % 2
                part = both[n_quad * QUAD : (n_quad + 1) * QUAD].reshape(HALF, HALF, tile)
                part = part * rho[a, j * HALF : (j + 1) * HALF, i * HALF : (i + 1) * HALF, at]
                part = jnp.sum(part, axis=0)
                keep = near[i] if b == 0 else jnp.logical_not(near[i])
                if row == 0:
                    keep = jnp.logical_and(keep, lat > 0)
                elif row == 3:
                    keep = jnp.logical_and(keep, lat < lats - 1)
                acc = acc + jnp.where(keep, part, 0.0)
            total[:, at] = acc

    add_piece(OWN, 0, [(1, 1), (2, 1), (1, 2), (2, 2)])

    for send in to_bands:
        send.wait_recv()
    add_piece(BAND, 0, [(0, 1), (0, 2), (3, 1), (3, 2)])
    for send in to_left:
        send.wait_recv()
    add_piece(RIGHT, 0, [(1, 3), (2, 3), (0, 3), (3, 3)])

    @pl.when(lon == 0)
    def _():
        send_left()

    for send in to_right[:2]:
        send.wait_recv()
    add_piece(LEFT, 2, [(0, 0), (3, 0)])
    for send, span in zip(to_right[2:], spans):
        send.wait_recv()
        add_piece(LEFT, 0, [(1, 0), (2, 0)], span)

    @pl.when(jnp.logical_not(leads))
    def _():
        pl.semaphore_wait(levs_in, 1)

    parts[lev] = jnp.sum(total[...], axis=0, keepdims=True)
    swaps = []
    for k in range(1, levs):
        swaps.append(
            pltpu.make_async_remote_copy(
                src_ref=parts.at[lev],
                dst_ref=parts.at[lev],
                send_sem=lev_send.at[k - 1],
                recv_sem=lev_recv.at[k - 1],
                device_id={"lev": wrapped(lev + k, levs)},
                device_id_type=MESH,
            )
        )
        swaps[-1].start()
    for swap in swaps:
        swap.wait_recv()
    value = parts[0]
    for k in range(1, levs):
        value = value + parts[k]
    for load in loads[6:]:
        load.wait()
    impact[...] = innovation[...] * inv_error[...] * value / (members - 1.0)

    for send in swaps + to_right + to_bands + to_left:
        send.wait_send()


def per_device(
    sizes,
    anomalies,
    error_grad,
    obs_lat,
    obs_lon,
    obs_level,
    obs_count,
    obs_pert,
    innovation,
    inv_error,
):
    rows, cols, width = anomalies.shape
    depth = error_grad.shape[2]
    members, slots = obs_pert.shape[2:]
    in_specs = [pl.BlockSpec(memory_space=pltpu.HBM)] * 9
    flat = (1, slots)
    impact = pl.pallas_call(
        functools.partial(kernel, sizes),
        out_shape=pltpu.VMEM(flat, jnp.float32),
        in_specs=in_specs,
        out_specs=pl.BlockSpec(memory_space=pltpu.VMEM),
        scratch_shapes=[
            pltpu.VMEM((rows, cols, width), jnp.bfloat16),
            pltpu.VMEM((rows, depth, cols), jnp.float32),
            pltpu.VMEM(flat, jnp.float32),
            pltpu.VMEM(flat, jnp.float32),
            pltpu.VMEM(flat, jnp.int32),
            pltpu.SMEM((1, 1), jnp.int32),
            pltpu.VMEM((members, slots), jnp.bfloat16),
            pltpu.VMEM(flat, jnp.float32),
            pltpu.VMEM(flat, jnp.float32),
            pltpu.VMEM((4, 4, QUAD, width), jnp.bfloat16),
            pltpu.VMEM((width, slots), jnp.bfloat16),
            pltpu.VMEM((2, rows, cols, slots), jnp.float32),
            pltpu.VMEM((HALF, slots), jnp.float32),
            pltpu.VMEM((sizes[0], 1, slots), jnp.float32),
            pltpu.SemaphoreType.DMA((9,)),
            pltpu.SemaphoreType.DMA((11,)),
            pltpu.SemaphoreType.DMA((11,)),
            pltpu.SemaphoreType.DMA((sizes[0] - 1,)),
            pltpu.SemaphoreType.DMA((sizes[0] - 1,)),
            pltpu.SemaphoreType.REGULAR,
            pltpu.SemaphoreType.REGULAR,
            pltpu.SemaphoreType.DMA((4,)),
        ],
        compiler_params=pltpu.CompilerParams(
            collective_id=0, has_side_effects=True, vmem_limit_bytes=58 * 1024 * 1024
        ),
        cost_estimate=pl.CostEstimate(
            flops=2 * 4 * rows * cols * width * slots, bytes_accessed=4 * 10**6, transcendentals=0
        ),
    )(
        anomalies,
        error_grad.transpose(0, 2, 1),
        obs_lat.reshape(flat),
        obs_lon.reshape(flat),
        obs_level.reshape(flat),
        obs_count,
        obs_pert.reshape(members, slots),
        innovation.reshape(flat),
        inv_error.reshape(flat),
    )
    return impact.reshape(1, 1, slots)


def solution(mesh):
    sizes = tuple(mesh.shape[a] for a in ("lev", "lat", "lon"))
    tiles = P("lat", "lon", None)
    placed = (
        P("lat", "lon", "lev"),
        P("lat", "lon", "lev"),
        tiles,
        tiles,
        tiles,
        P("lat", "lon"),
        P("lat", "lon", None, None),
        tiles,
        tiles,
    )
    return jax.shard_map(
        functools.partial(per_device, sizes),
        mesh=mesh,
        in_specs=placed,
        out_specs=tiles,
        check_vma=False,
    )
```
